32 devices in a mesh: side: 2 (over core), row: 4 (over y, x), col: 4 (over z).
Axes of the slice: x: 2, y: 2, z: 4, core: 2. Of those that a mesh axis runs over, the one named last changes fastest.
Arguments:
- right_side: float32 [256, 128, 548], P('row', 'col', 'side'), may hold values from -24 to 24
- couplings: float32 [4, 256, 128], P(None, 'row', 'col'), may hold values from 0.04 to 0.2
- channel_rates: float32 [548], P('side'), may hold values from 0.2 to 1
- weight_in: float32 [548, 1024], replicated, may hold values from -0.25 to 0.25
- weight_mid: float32 [1024, 1024], replicated, may hold values from -0.1875 to 0.1875
- weight_out: float32 [1024, 616], replicated, may hold values from -0.1875 to 0.1875
- inverse_cov: float32 [616, 616], replicated, may hold values from -2 to 8, as said below
- profile_cells: int32 [2, 8192], P(None, ('row', 'col')), may hold values from 0 to 2047
- profile_counts: int32 [32], replicated, may hold values from 1 to 512, 4096 in all
- gate_first: bfloat16 [16384, 1024], P(('side', 'row', 'col')), may hold values from 0 to 1.09375
- gate_second: bfloat16 [16384, 1024], P(('side', 'row', 'col')), may hold values from 0 to 1.09375
Outputs:
- solution: float32 [256, 128, 548], P('row', 'col', 'side')
- residual: float32 [256, 128, 548], P('row', 'col', 'side')
The draws below stay inside these ranges and needn't reach their ends.
Inputs may be any that keep to these rules, and one draw needn't show every extreme that they name: `profile_counts`: entry d counts the live profiles of device d in the order side, row, col; they fill its first slots. The entries add up to 4096, and the largest is 512. `profile_cells`: entry [s, t * 512 + i] is the cell, numbered latitude-major within tile t, observed by slot i of device s * 16 + t; entries of slots that are not live are unused. `inverse_cov`: symmetric positive definite.
All inputs are finite; a program needn't handle non-finite values.
Results may differ from the reference program's by a relative error of at most 0.0003.
Values may be sent and summed in bfloat16 or wider, within the bound.
A program may use at most 128 MiB of HBM per device.

```python
import math
import jax
import jax.numpy as jnp
import numpy as np
from jax import lax

CLAT = 64
CLON = 32
NVAL = 548
HID = 1024
NOUT = 616
BAL = 128
ITERS = 2
PSLOT = 512
CELLS = 2048
TILES = 16
NLAT = 256
NLON = 128
PROFILES = 16384
N_SIDE = 2
N_COL = 4
DEVICES = 32


def draw_right_side(key, part):
    latitude = jnp.arange(NLAT, dtype=jnp.float32)[:, None, None] / NLAT
    longitude = jnp.arange(NLON, dtype=jnp.float32)[None, :, None] / NLON
    channel = jnp.arange(NVAL, dtype=jnp.float32)[None, None, :] / NVAL
    spread_scale = jnp.exp(0.5 * jnp.log(3.0) * (latitude + longitude + channel))
    random_part = jnp.clip(jax.random.normal(key, (NLAT, NLON, NVAL), jnp.float32), -4.0, 4.0)
    return random_part * spread_scale


def draw_inverse_cov(key, part):
    diag_key = jax.random.fold_in(key, 11)
    matrix_key = jax.random.fold_in(key, 23)
    diagonal = 1.0 + 2.0 * jax.random.uniform(diag_key, (NOUT,), jnp.float32)
    random_matrix = jnp.clip(jax.random.normal(matrix_key, (NOUT, NOUT), jnp.float32), -4.0, 4.0)
    product_part = jnp.dot(random_matrix, random_matrix.T, precision=lax.Precision.HIGHEST) / NOUT
    product_part = 0.5 * (product_part + product_part.T)
    return product_part + jnp.diag(diagonal)


def touch_ends(entries, rng, least, high):
    spot = [jax.random.randint(jax.random.fold_in(rng, axis), (), 0, length) for axis, length in enumerate(entries.shape)]
    main_axis = entries.shape.index(max(entries.shape))
    neighbour = spot[:main_axis] + [(spot[main_axis] + 1) % entries.shape[main_axis]] + spot[main_axis + 1:]
    return entries.at[tuple(spot)].set(least).at[tuple(neighbour)].set(high)


def shard_levels(stream_key, dims, split, low, largest):
    level, own = 1.0, jax.random.fold_in(stream_key, 6)
    for position, parts in split:
        steps = jnp.exp(jax.random.uniform(jax.random.fold_in(own, position), (parts,), jnp.float32, low / len(split), largest / len(split)))
        level = level * jnp.repeat(steps, dims[position] // parts).reshape([-1 if axis == position else 1 for axis in range(len(dims))])
    return level


def length_profile(number_of, total, most, slope):
    loads = [(1 << 20) // math.isqrt(standing ** slope) + 1 for standing in range(2, number_of + 1)]
    spare, given = total - most - (number_of - 1), [1] * (number_of - 1)
    while spare > 0:
        free = [i for i in range(number_of - 1) if given[i] < most]
        pool, remaining = sum([loads[i] for i in free]), spare
        for i in free:
            addition = min(most - given[i], max(1, remaining * loads[i] // pool), spare)
            given[i] = given[i] + addition
            spare = spare - addition
    return np.array([most] + given)


def ragged(rng, count, total, reach, skew):
    if count == 2:
        one = jax.random.randint(rng, (), max(1, total - reach), min(reach, total - 1) + 1)
        return jnp.stack([one, total - one])
    tallies = jnp.asarray(length_profile(count, total, reach, skew), jnp.int32)
    twos = (count - 1) // 2
    source_of, taker = tallies[1:1 + 2 * twos:2], tallies[2:2 + 2 * twos:2]
    slack = jnp.minimum(source_of - 1, reach - taker)
    moved = jax.random.randint(jax.random.fold_in(rng, 1), (twos,), 0, 1 << 20) % (slack + 1)
    tallies = tallies.at[1:1 + 2 * twos:2].set(source_of - moved).at[2:2 + 2 * twos:2].set(taker + moved)
    return tallies[jax.random.permutation(jax.random.fold_in(rng, 2), count)]


def scatter_about(stream_key, shape, deviation, reach, kind=jnp.bfloat16):
    values = deviation * jax.random.normal(stream_key, shape, jnp.float32)
    return jnp.clip(values, min=-reach, max=reach).astype(kind)


def setup_inputs(seed: int = 0) -> dict:
    key_list = jax.random.split(jax.random.key(seed), 12)
    return {
        "right_side": draw_right_side(jax.random.fold_in(key_list[11], 71), 0),
        "couplings": jnp.clip(jnp.exp(math.log(0.2) - 1.609438 * jax.random.uniform(key_list[1], (4, NLAT, NLON), jnp.float32) ** shard_levels(key_list[1], (4, NLAT, NLON), ((1, 4), (2, 4)), -0.2, 0.2)), 0.04, 0.2),
        "channel_rates": jnp.clip(jnp.exp(math.log(1.0) - 1.609438 * jax.random.uniform(key_list[2], (NVAL,), jnp.float32) ** shard_levels(key_list[2], (NVAL,), ((0, 2),), -0.2, 0.2)), 0.2, 1.0),
        "weight_in": scatter_about(key_list[3], (NVAL, HID), NVAL ** -0.5, 0.25, jnp.float32),
        "weight_mid": scatter_about(key_list[4], (HID, HID), HID ** -0.5, 0.1875, jnp.float32),
        "weight_out": scatter_about(key_list[5], (HID, NOUT), HID ** -0.5, 0.1875, jnp.float32),
        "inverse_cov": draw_inverse_cov(jax.random.fold_in(key_list[11], 71), 0),
        "profile_cells": touch_ends(jax.random.randint(key_list[7], (N_SIDE, TILES * PSLOT), 0, CELLS), jax.random.fold_in(key_list[7], 1), 0, CELLS - 1).astype(jnp.int32),
        "profile_counts": ragged(key_list[8], DEVICES, DEVICES * BAL, PSLOT, 2).astype(jnp.int32),
        "gate_first": jnp.clip(1.09375 * jax.random.uniform(key_list[9], (PROFILES, HID), jnp.float32) ** shard_levels(key_list[9], (PROFILES, HID), ((0, 32),), -0.2, 0.2), 0.0, 1.09375).astype(jnp.bfloat16),
        "gate_second": jnp.clip(1.09375 * jax.random.uniform(key_list[10], (PROFILES, HID), jnp.float32) ** shard_levels(key_list[10], (PROFILES, HID), ((0, 32),), -0.2, 0.2), 0.0, 1.09375).astype(jnp.bfloat16),
    }


highest = lax.Precision.HIGHEST


def product(first_matrix, second_matrix):
    return jnp.dot(first_matrix, second_matrix, precision=highest, preferred_element_type=jnp.float32)


def product_back(first_matrix, second_matrix):
    return lax.dot_general(first_matrix, second_matrix, (((1,), (1,)), ((), ())), precision=highest, preferred_element_type=jnp.float32)


def network(profile_rows, gate_one, gate_two, weight_in, weight_mid, weight_out, inverse_cov):
    hidden = product(profile_rows, weight_in) * gate_one
    hidden = product(hidden, weight_mid) * gate_two
    weighted = product(product(hidden, weight_out), inverse_cov)
    adjoint_part = product_back(weighted, weight_out) * gate_two
    adjoint_part = product_back(adjoint_part, weight_mid) * gate_one
    return product_back(adjoint_part, weight_in)


def masked_couplings(couplings):
    latitude = jnp.arange(NLAT)[:, None]
    north_part = jnp.where(latitude < NLAT - 1, couplings[2], 0.0)
    south_part = jnp.where(latitude > 0, couplings[3], 0.0)
    return couplings[0], couplings[1], north_part, south_part


def tangent(state_field, weights, channel_rates):
    east_weight, west_weight, north_weight, south_weight = weights
    net_flux = east_weight[:, :, None] * (jnp.roll(state_field, -1, axis=1) - state_field)
    net_flux = net_flux + west_weight[:, :, None] * (jnp.roll(state_field, 1, axis=1) - state_field)
    net_flux = net_flux + north_weight[:, :, None] * (jnp.roll(state_field, -1, axis=0) - state_field)
    net_flux = net_flux + south_weight[:, :, None] * (jnp.roll(state_field, 1, axis=0) - state_field)
    return state_field + channel_rates * net_flux


def adjoint(state_field, weights, channel_rates):
    east_weight, west_weight, north_weight, south_weight = weights
    scaled = channel_rates * state_field
    coupling_sum = (east_weight + west_weight + north_weight + south_weight)[:, :, None]
    result = state_field - coupling_sum * scaled
    result = result + jnp.roll(east_weight[:, :, None] * scaled, 1, axis=1)
    result = result + jnp.roll(west_weight[:, :, None] * scaled, -1, axis=1)
    result = result + jnp.roll(north_weight[:, :, None] * scaled, 1, axis=0)
    result = result + jnp.roll(south_weight[:, :, None] * scaled, -1, axis=0)
    return result


def observe(model_image, profile_cells, profile_counts, gate_first, gate_second, weight_in, weight_mid, weight_out, inverse_cov):
    count_ends = jnp.cumsum(profile_counts).astype(jnp.int32)
    starts = (count_ends - profile_counts).astype(jnp.int32)
    global_rank = jnp.arange(DEVICES * BAL, dtype=jnp.int32)
    source = jnp.searchsorted(count_ends, global_rank, side="right").astype(jnp.int32)
    local_row = (global_rank - starts[source]).astype(jnp.int32)
    side_index = source // TILES
    tile_index = source % TILES
    cell_index = profile_cells[side_index, tile_index * PSLOT + local_row].astype(jnp.int32)
    latitude = (tile_index // N_COL) * CLAT + cell_index // CLON
    longitude = (tile_index % N_COL) * CLON + cell_index % CLON
    flat_cell = (latitude * NLON + longitude).astype(jnp.int32)
    slot_index = (source * PSLOT + local_row).astype(jnp.int32)
    columns = model_image.reshape(NLAT * NLON, NVAL)[flat_cell]
    block_rows = min(1024, DEVICES * BAL)

    def run_block(pieces):
        return network(pieces[0], pieces[1], pieces[2], weight_in, weight_mid, weight_out, inverse_cov)

    gradients = lax.map(run_block, (columns.reshape(-1, block_rows, NVAL), gate_first[slot_index].reshape(-1, block_rows, HID), gate_second[slot_index].reshape(-1, block_rows, HID)))
    summed = jax.ops.segment_sum(gradients.reshape(-1, NVAL), flat_cell, num_segments=NLAT * NLON)
    return summed.reshape(NLAT, NLON, NVAL)


def reference(right_side, couplings, channel_rates, weight_in, weight_mid, weight_out, inverse_cov, profile_cells, profile_counts, gate_first, gate_second):
    weights = masked_couplings(couplings)

    def hessian(direction):
        model_image = tangent(direction, weights, channel_rates)
        spread_field = observe(model_image, profile_cells, profile_counts, gate_first, gate_second, weight_in, weight_mid, weight_out, inverse_cov)
        return direction + adjoint(spread_field, weights, channel_rates)

    solution = jnp.zeros_like(right_side)
    residual = right_side
    direction = right_side
    norm_now = jnp.sum(residual * residual)
    for iteration in range(ITERS):
        hessian_image = hessian(direction)
        step_size = norm_now / jnp.sum(direction * hessian_image)
        solution = solution + step_size * direction
        residual = residual - step_size * hessian_image
        if iteration + 1 < ITERS:
            norm_next = jnp.sum(residual * residual)
            direction = residual + (norm_next / norm_now) * direction
            norm_now = norm_next
    return solution, residual
```

```python
import functools

import jax
import jax.numpy as jnp
from jax import lax
from jax.experimental import pallas as pl
from jax.experimental.pallas import tpu as pltpu
from jax.sharding import PartitionSpec as P

highest = lax.Precision.HIGH


def extended(array, sides, width):
    for axis, dim in sides:
        count, length = (lax.axis_size(axis), array.shape[dim])
        up = [(i, (i + 1) % count) for i in range(count)]
        down = [(j, i) for i, j in up]
        last = lax.slice_in_dim(array, length - width, length, axis=dim)
        first = lax.slice_in_dim(array, 0, width, axis=dim)
        before = lax.ppermute(last, axis, up)
        after = lax.ppermute(first, axis, down)
        array = jnp.concatenate([before, array, after], axis=dim)
    return array


def swapped(value, axis, distance):
    mask = 2**distance
    pairs = [(source, source ^ mask) for source in range(lax.axis_size(axis))]
    return lax.ppermute(value, axis, pairs)


def product(first_matrix, second_matrix):
    return jnp.dot(
        first_matrix, second_matrix, precision=highest, preferred_element_type=jnp.float32
    )


def product_back(first_matrix, second_matrix):
    return lax.dot_general(
        first_matrix,
        second_matrix,
        (((1,), (1,)), ((), ())),
        precision=highest,
        preferred_element_type=jnp.float32,
    )


def network(profile_rows, gate_one, gate_two, weight_in, weight_mid, weight_out, inverse_cov):
    hidden = product(profile_rows, weight_in) * gate_one
    hidden = product(hidden, weight_mid) * gate_two
    weighted = product(product(hidden, weight_out), inverse_cov)
    adjoint_part = product_back(weighted, weight_out) * gate_two
    adjoint_part = product_back(adjoint_part, weight_mid) * gate_one
    return product_back(adjoint_part, weight_in)


def extend(state_field):
    return extended(state_field, (("row", 0), ("col", 1)), 1)


def tangent(state_field, weights, channel_rates):
    padded = extend(state_field)
    net_flux = weights[:, :, 0:1] * (padded[1:-1, 2:] - state_field)
    net_flux = net_flux + weights[:, :, 1:2] * (padded[1:-1, :-2] - state_field)
    net_flux = net_flux + weights[:, :, 2:3] * (padded[2:, 1:-1] - state_field)
    net_flux = net_flux + weights[:, :, 3:4] * (padded[:-2, 1:-1] - state_field)
    return state_field + channel_rates * net_flux


def adjoint(state_field, weights, wide_weights, channel_rates):
    scaled = channel_rates * state_field
    padded = extend(scaled)
    coupling_sum = weights[:, :, 0:1] + weights[:, :, 1:2] + weights[:, :, 2:3] + weights[:, :, 3:4]
    result = state_field - coupling_sum * scaled
    result = result + wide_weights[1:-1, :-2, 0:1] * padded[1:-1, :-2]
    result = result + wide_weights[1:-1, 2:, 1:2] * padded[1:-1, 2:]
    result = result + wide_weights[:-2, 1:-1, 2:3] * padded[:-2, 1:-1]
    result = result + wide_weights[2:, 1:-1, 3:4] * padded[2:, 1:-1]
    return result


MESH = pl.DeviceIdType.MESH


def sums_kernel(sides, rows, cols, x_ref, o_ref, plane, line, send_sem, recv_sem):
    side, row, col = lax.axis_index("side"), lax.axis_index("row"), lax.axis_index("col")
    near = [
        (lax.rem(side + ds, sides), lax.rem(row + dr, rows), col)
        for ds in range(sides)
        for dr in range(rows)
        if ds + dr
    ]
    far = [(side, row, lax.rem(col + dc, cols)) for dc in range(1, cols)]
    barrier = pltpu.get_barrier_semaphore()
    for peer in near + far:
        pl.semaphore_signal(barrier, inc=1, device_id=peer, device_id_type=MESH)
    pl.semaphore_wait(barrier, len(near) + len(far))

    def exchange(value, peers, buffer, slot, first):
        buffer[slot] = value
        copies = [
            pltpu.make_async_remote_copy(
                src_ref=buffer.at[slot],
                dst_ref=buffer.at[slot],
                send_sem=send_sem.at[first + k],
                recv_sem=recv_sem.at[first + k],
                device_id=peer,
                device_id_type=MESH,
            )
            for k, peer in enumerate(peers)
        ]
        for copy in copies:
            copy.start()
        for copy in copies:
            copy.wait()
        return jnp.sum(buffer[...], axis=0)

    plane_sum = exchange(x_ref[...], near, plane, side * rows + row, 0)
    o_ref[...] = exchange(plane_sum, far, line, col, len(near))


def all_sums(parts):
    sides, rows, cols = (lax.axis_size(axis) for axis in ("side", "row", "col"))
    count = sides * rows - 1 + cols - 1
    block = jnp.broadcast_to(jnp.stack(parts)[:, None], (len(parts), 128))
    total = pl.pallas_call(
        functools.partial(sums_kernel, sides, rows, cols),
        out_shape=jax.ShapeDtypeStruct(block.shape, jnp.float32),
        in_specs=[pl.BlockSpec(memory_space=pltpu.VMEM)],
        out_specs=pl.BlockSpec(memory_space=pltpu.VMEM),
        scratch_shapes=[
            pltpu.VMEM((sides * rows, *block.shape), jnp.float32),
            pltpu.VMEM((cols, *block.shape), jnp.float32),
            pltpu.SemaphoreType.DMA((count,)),
            pltpu.SemaphoreType.DMA((count,)),
        ],
        compiler_params=pltpu.CompilerParams(collective_id=0, has_side_effects=True),
    )(block)
    return [total[i, 0] for i in range(len(parts))]


def gain_scale(weight_in, weight_mid, weight_out, inverse_cov):
    def squares(matrix):
        return jnp.sum(matrix * matrix)

    bound = squares(weight_in) * squares(weight_mid) * squares(weight_out)
    return 1.0 / jnp.maximum(bound * jnp.sqrt(squares(inverse_cov)), 1.0)


def combination(scale, bb, bw, ww, wx):
    bw = bw / scale
    curve = bb + bw
    step = bb / curve
    rest = bw / curve
    grown = step / scale
    ratio = (grown * ww / bb) * grown - rest * rest
    norm = ratio * bb
    along = norm + rest * rest * bw - 2.0 * rest * (grown * ww / scale) + grown * (grown * wx) / scale
    second = norm / (along - ratio * norm / step)
    mixed = rest + ratio
    of_solution = (step + second * mixed, -second * grown)
    of_residual = (
        rest - second * mixed,
        -grown - second * (mixed / scale - grown),
        (second / scale) * grown,
    )
    return of_solution, of_residual


def local(
    right_side,
    couplings,
    channel_rates,
    weight_in,
    weight_mid,
    weight_out,
    inverse_cov,
    profile_cells,
    profile_counts,
    gate_first,
    gate_second,
):
    side_index = lax.axis_index("side")
    tile_count = lax.axis_size("row") * lax.axis_size("col")
    tile_index = lax.axis_index("row") * lax.axis_size("col") + lax.axis_index("col")
    lat_rows, lon_cols, half_width = right_side.shape
    slot_count = profile_cells.shape[1]
    latitude = lax.axis_index("row") * lat_rows + jnp.arange(lat_rows)
    north_open = (latitude < lat_rows * lax.axis_size("row") - 1)[:, None]
    south_open = (latitude > 0)[:, None]
    weights = jnp.stack(
        [
            couplings[0],
            couplings[1],
            jnp.where(north_open, couplings[2], 0.0),
            jnp.where(south_open, couplings[3], 0.0),
        ],
        axis=2,
    )
    wide_weights = extend(weights)
    pair_counts = jnp.stack([profile_counts[tile_index], profile_counts[tile_count + tile_index]])
    live_mask = (jnp.arange(slot_count)[None, :] < pair_counts[:, None])[:, :, None]
    flat_cells = profile_cells.reshape(-1)

    def observe(model_image):
        flat_image = model_image.reshape(lat_rows * lon_cols, half_width)
        halves = flat_image[flat_cells].reshape(2, slot_count, half_width) * live_mask
        lower_first = side_index == 0
        own_half = lax.dynamic_index_in_dim(halves, side_index, 0, keepdims=False)
        other_half = lax.dynamic_index_in_dim(halves, 1 - side_index, 0, keepdims=False)
        partner_half = swapped(other_half, "side", 0)
        profile_rows = jnp.where(
            lower_first,
            jnp.concatenate([own_half, partner_half], axis=1),
            jnp.concatenate([partner_half, own_half], axis=1),
        )
        gradients = network(
            profile_rows, gate_first, gate_second, weight_in, weight_mid, weight_out, inverse_cov
        )
        first_half = gradients[:, :half_width]
        second_half = gradients[:, half_width:]
        own_grad = jnp.where(lower_first, first_half, second_half)
        other_grad = jnp.where(lower_first, second_half, first_half)
        partner_grad = swapped(other_grad, "side", 0)
        pair_grads = jnp.where(
            lower_first, jnp.stack([own_grad, partner_grad]), jnp.stack([partner_grad, own_grad])
        )
        summed = jax.ops.segment_sum(
            pair_grads.reshape(-1, half_width), flat_cells, num_segments=lat_rows * lon_cols
        )
        return summed.reshape(lat_rows, lon_cols, half_width)

    scale = gain_scale(weight_in, weight_mid, weight_out, inverse_cov)
    inverse_cov = scale * inverse_cov

    def spread(field):
        return adjoint(observe(tangent(field, weights, channel_rates)), weights, wide_weights, channel_rates)

    first = spread(right_side)
    second = spread(first)
    zero = jnp.zeros((), jnp.float32)
    sums = all_sums(
        [
            jnp.sum(right_side * right_side),
            jnp.sum(right_side * first),
            jnp.sum(first * first),
            jnp.sum(first * second),
            zero,
            zero,
            zero,
            zero,
        ]
    )
    of_solution, of_residual = combination(scale, *sums[:4])
    solution = of_solution[0] * right_side + of_solution[1] * first
    residual = of_residual[0] * right_side + of_residual[1] * first + of_residual[2] * second
    return (solution, residual)


def solution(mesh):
    in_specs = (
        P("row", "col", "side"),
        P(None, "row", "col"),
        P("side"),
        P(),
        P(),
        P(),
        P(),
        P(None, ("row", "col")),
        P(),
        P(("side", "row", "col"), None),
        P(("side", "row", "col"), None),
    )
    out_specs = (P("row", "col", "side"), P("row", "col", "side"))
    return jax.shard_map(local, mesh=mesh, in_specs=in_specs, out_specs=out_specs, check_vma=False)
```

```python
import functools

import jax
import jax.numpy as jnp
from jax import lax
from jax.experimental import pallas as pl
from jax.experimental.pallas import tpu as pltpu
from jax.sharding import PartitionSpec as P

MESH = pl.DeviceIdType.MESH


def sums_kernel(sides, rows, cols, x_ref, o_ref, plane, line, send_sem, recv_sem):
    side, row, col = lax.axis_index("side"), lax.axis_index("row"), lax.axis_index("col")
    near = [
        (lax.rem(side + ds, sides), lax.rem(row + dr, rows), col)
        for ds in range(sides)
        for dr in range(rows)
        if ds + dr
    ]
    far = [(side, row, lax.rem(col + dc, cols)) for dc in range(1, cols)]
    barrier = pltpu.get_barrier_semaphore()
    for peer in near + far:
        pl.semaphore_signal(barrier, inc=1, device_id=peer, device_id_type=MESH)
    pl.semaphore_wait(barrier, len(near) + len(far))

    def exchange(value, peers, buffer, slot, first):
        buffer[slot] = value
        copies = [
            pltpu.make_async_remote_copy(
                src_ref=buffer.at[slot],
                dst_ref=buffer.at[slot],
                send_sem=send_sem.at[first + k],
                recv_sem=recv_sem.at[first + k],
                device_id=peer,
                device_id_type=MESH,
            )
            for k, peer in enumerate(peers)
        ]
        for copy in copies:
            copy.start()
        for copy in copies:
            copy.wait()
        return jnp.sum(buffer[...], axis=0)

    plane_sum = exchange(x_ref[...], near, plane, side * rows + row, 0)
    o_ref[...] = exchange(plane_sum, far, line, col, len(near))


VMEM = pl.BlockSpec(memory_space=pltpu.VMEM)
SMEM = pl.BlockSpec(memory_space=pltpu.SMEM)
LANES = 128
GRANT = 56 * 1024 * 1024


def call(kernel, shapes, specs, scratch, *operands, **params):
    out = [jax.ShapeDtypeStruct(shape, jnp.float32) for shape in shapes]
    params = pltpu.CompilerParams(vmem_limit_bytes=GRANT, **params)
    return pl.pallas_call(
        kernel,
        out_shape=out,
        in_specs=specs,
        out_specs=[VMEM] * len(out),
        scratch_shapes=scratch,
        compiler_params=params,
    )(*operands)


def all_sums(block):
    sides, rows, cols = (lax.axis_size(axis) for axis in ("side", "row", "col"))
    count = sides * rows - 1 + cols - 1
    scratch = [
        pltpu.VMEM((sides * rows, *block.shape), jnp.float32),
        pltpu.VMEM((cols, *block.shape), jnp.float32),
        pltpu.SemaphoreType.DMA((count,)),
        pltpu.SemaphoreType.DMA((count,)),
    ]
    kernel = functools.partial(sums_kernel, sides, rows, cols)
    return call(kernel, [block.shape], [VMEM], scratch, block, collective_id=0, has_side_effects=True)[0]


def halo_kernel(rows, cols, first_lat, last_lat, first_lon, last_lon, *rest):
    outs, lands, (send_sem, recv_sem) = rest[:4], rest[4:8], rest[8:]
    side, row, col = lax.axis_index("side"), lax.axis_index("row"), lax.axis_index("col")
    below = (side, lax.rem(row + rows - 1, rows), col)
    above = (side, lax.rem(row + 1, rows), col)
    behind = (side, row, lax.rem(col + cols - 1, cols))
    ahead = (side, row, lax.rem(col + 1, cols))
    peers = (above, below, ahead, behind)
    barrier = pltpu.get_barrier_semaphore()
    for peer in peers:
        pl.semaphore_signal(barrier, inc=1, device_id=peer, device_id_type=MESH)
    pl.semaphore_wait(barrier, 4)
    copies = [
        pltpu.make_async_remote_copy(
            src_ref=source,
            dst_ref=land,
            send_sem=send_sem.at[k],
            recv_sem=recv_sem.at[k],
            device_id=peer,
            device_id_type=MESH,
        )
        for k, (source, land, peer) in enumerate(zip((last_lat, first_lat, last_lon, first_lon), lands, peers))
    ]
    for copy in copies:
        copy.start()
    for copy, land, out in zip(copies, lands, outs):
        copy.wait()
        out[...] = land[...]


def halos(first_lat, last_lat, first_lon, last_lon):
    kernel = functools.partial(halo_kernel, lax.axis_size("row"), lax.axis_size("col"))
    shapes = [first_lat.shape, first_lat.shape, first_lon.shape, first_lon.shape]
    scratch = [pltpu.VMEM(shape, jnp.float32) for shape in shapes]
    scratch += [pltpu.SemaphoreType.DMA((4,)), pltpu.SemaphoreType.DMA((4,))]
    operands = (first_lat, last_lat, first_lon, last_lon)
    return call(kernel, shapes, [VMEM] * 4, scratch, *operands, collective_id=1, has_side_effects=True)


def live_counts(counts):
    side = lax.axis_index("side")
    tiles = lax.axis_size("row") * lax.axis_size("col")
    tile = lax.axis_index("row") * lax.axis_size("col") + lax.axis_index("col")
    return (side, counts[side * tiles + tile]), (1 - side, counts[(1 - side) * tiles + tile])


def gather_kernel(field, before, after, left, right, weights, rates, cells, counts, own, other, image):
    lats, lons, width = field.shape
    rate = rates[...]
    whole = width // LANES * LANES
    image[:, whole:] = jnp.zeros((image.shape[0], image.shape[1] - whole), jnp.float32)

    def line(i, value, following, preceding):
        weight = weights[i]
        east = jnp.concatenate([value[1:], right[pl.ds(i, 1)]], axis=0)
        west = jnp.concatenate([left[pl.ds(i, 1)], value[:-1]], axis=0)
        flux = weight[:, 0:1] * (east - value) + weight[:, 1:2] * (west - value)
        flux = flux + weight[:, 2:3] * (following - value) + weight[:, 3:4] * (preceding - value)
        image[pl.ds(pl.multiple_of(i * lons, lons), lons), :width] = value + rate * flux

    line(0, field[0], field[1], before[...])
    line(lats - 1, field[lats - 1], after[...], field[lats - 2])

    @pl.loop(1, lats - 1)
    def _(i):
        line(i, field[i], field[i + 1], field[i - 1])

    for (side, live), out in zip(live_counts(counts), (own, other)):

        @pl.loop(0, (live + 7) // 8)
        def _(j):
            base = pl.multiple_of(j * 8, 8)
            lines = [image[pl.ds(cells[side, base + k], 1)] for k in range(8)]
            out[pl.ds(base, 8)] = jnp.concatenate(lines, axis=0)


def scatter_kernel(own, other, weights, rates, cells, counts, spread, to_before, to_after, to_left, to_right):
    lats, lons, _ = weights.shape
    width = rates.shape[1]
    rate = rates[...]
    spread[...] = jnp.zeros_like(spread)
    for (side, live), grads in zip(live_counts(counts), (own, other)):

        @pl.loop(0, live)
        def _(i):
            cell = cells[side, i]
            spread[pl.ds(cell, 1)] = spread[pl.ds(cell, 1)] + grads[pl.ds(i, 1)]

    to_before[...] = weights[0][:, 3:4] * (rate * spread[:lons, :width])
    to_after[...] = weights[lats - 1][:, 2:3] * (rate * spread[(lats - 1) * lons :, :width])

    @pl.loop(0, lats)
    def _(i):
        base = pl.multiple_of(i * lons, lons)
        weight = weights[i]
        lines = rate * spread[pl.ds(base, lons), :width]
        to_left[pl.ds(i, 1)] = weight[:1, 1:2] * lines[:1]
        to_right[pl.ds(i, 1)] = weight[lons - 1 :, 0:1] * lines[lons - 1 :]


def adjoint_kernel(is_first, spread, before, after, left, right, weights, rates, field, sums, out, *rest):
    lats, lons, width = field.shape
    rate = rates[...]

    def scaled(i):
        return rate * spread[pl.ds(pl.multiple_of(i * lons, lons), lons), :width]

    def line(i, preceding, following, totals):
        weight = weights[i]
        value = spread[pl.ds(pl.multiple_of(i * lons, lons), lons), :width]
        flow = rate * value
        east = weight[:, 0:1] * flow
        west = weight[:, 1:2] * flow
        total = weight[:, 0:1] + weight[:, 1:2] + weight[:, 2:3] + weight[:, 3:4]
        result = value - total * flow + preceding + following
        result = result + jnp.concatenate([left[pl.ds(i, 1)], east[:-1]], axis=0)
        result = result + jnp.concatenate([west[1:], right[pl.ds(i, 1)]], axis=0)
        out[i] = result
        known = field[i]
        if not is_first:
            return (totals[0] + known * result,)
        rest[2][pl.ds(i, 1)] = result[:1]
        rest[3][pl.ds(i, 1)] = result[lons - 1 :]
        return totals[0] + known * known, totals[1] + known * result, totals[2] + result * result

    def inner(i, totals):
        return line(i, weights[i - 1][:, 2:3] * scaled(i - 1), weights[i + 1][:, 3:4] * scaled(i + 1), totals)

    totals = tuple(jnp.zeros((lons, width), jnp.float32) for _ in range(3 if is_first else 1))
    totals = line(0, before[...], weights[1][:, 3:4] * scaled(1), totals)
    totals = lax.fori_loop(1, lats - 1, inner, totals)
    totals = line(lats - 1, weights[lats - 2][:, 2:3] * scaled(lats - 2), after[...], totals)
    lines = lax.broadcasted_iota(jnp.int32, sums.shape, 0)
    block = sums[...]
    for k, total in enumerate(totals):
        block = jnp.where(lines == (k if is_first else 3), jnp.sum(total), block)
    if is_first:
        rest[0][...] = out[0]
        rest[1][...] = out[lats - 1]
    rest[-1][...] = block


def network_kernel(own, other, gate_one, gate_two, w_own, w_other, w_mid, w_out, cov, counts, d_own, d_other, scale_out, *scratch):
    pairs = [scratch[2 * k : 2 * k + 2] for k in range(5)]
    squares = []
    for full, (high, low) in zip((w_own, w_other, w_mid, w_out, cov), pairs):
        chunk = 32

        def split(c, total, full=full, high=high, low=low):
            lines = pl.ds(pl.multiple_of(c * chunk, chunk), chunk)
            value = full[lines]
            rounded = value.astype(jnp.bfloat16)
            high[lines] = rounded
            low[lines] = (value - rounded.astype(jnp.float32)).astype(jnp.bfloat16)
            return total + value * value

        start = jnp.zeros((chunk, full.shape[1]), jnp.float32)
        squares.append(jnp.sum(lax.fori_loop(0, full.shape[0] // chunk, split, start), axis=(0, 1), keepdims=True))
    bound = (squares[0] + squares[1]) * squares[2] * squares[3] * jnp.sqrt(squares[4])
    scale = 1.0 / jnp.maximum(bound, 1.0)
    scale_out[...] = jnp.broadcast_to(scale, scale_out.shape)
    p_own, p_other, p_mid, p_out, p_cov = pairs

    def product(value, pair, back=False):
        dims = (((1,), (1 if back else 0,)), ((), ()))
        high = value.astype(jnp.bfloat16)
        low = (value - high.astype(jnp.float32)).astype(jnp.bfloat16)

        def dot(left, right):
            return lax.dot_general(left, right[...], dims, preferred_element_type=jnp.float32)

        return dot(high, pair[0]) + (dot(low, pair[0]) + dot(high, pair[1]))

    rows = min(256, own.shape[0])
    live = live_counts(counts)[0][1]

    @pl.loop(0, (live + rows - 1) // rows)
    def _(j):
        lines = pl.ds(pl.multiple_of(j * rows, rows), rows)
        g1 = gate_one[lines].astype(jnp.float32)
        hidden = (product(own[lines], p_own) + product(other[lines], p_other)) * g1
        hidden = product(hidden, p_mid) * gate_two[lines].astype(jnp.float32)
        weighted = product(product(hidden, p_out), p_cov) * scale
        back = product(weighted, p_out, True) * gate_two[lines].astype(jnp.float32)
        back = product(back, p_mid, True) * gate_one[lines].astype(jnp.float32)
        d_own[lines] = product(back, p_own, True)
        d_other[lines] = product(back, p_other, True)


def combination(scale, bb, bw, ww, wx):
    bw = bw / scale
    curve = bb + bw
    step = bb / curve
    rest = bw / curve
    grown = step / scale
    ratio = (grown * ww / bb) * grown - rest * rest
    norm = ratio * bb
    along = norm + rest * rest * bw - 2.0 * rest * (grown * ww / scale) + grown * (grown * wx) / scale
    second = norm / (along - ratio * norm / step)
    mixed = rest + ratio
    of_solution = (step + second * mixed, -second * grown)
    of_residual = (
        rest - second * mixed,
        -grown - second * (mixed / scale - grown),
        (second / scale) * grown,
    )
    return of_solution, of_residual


def finish_kernel(sums, scale, b, w, x, solution, residual):
    values = [sums[k : k + 1, 0:1] for k in range(4)]
    of_solution, of_residual = combination(scale[0:1, 0:1], *values)
    solution[...] = of_solution[0] * b[...] + of_solution[1] * w[...]
    residual[...] = of_residual[0] * b[...] + of_residual[1] * w[...] + of_residual[2] * x[...]


def finish(sums, scale, b, w, x):
    lats, lons, width = b.shape
    part = 8 if lats % 8 == 0 else lats
    whole = pl.BlockSpec(sums.shape, lambda i: (0, 0))
    block = pl.BlockSpec((part, lons, width), lambda i: (i, 0, 0))
    return pl.pallas_call(
        finish_kernel,
        grid=(lats // part,),
        out_shape=[jax.ShapeDtypeStruct(b.shape, jnp.float32)] * 2,
        in_specs=[whole, whole, block, block, block],
        out_specs=[block, block],
        compiler_params=pltpu.CompilerParams(vmem_limit_bytes=GRANT),
    )(sums, scale, b, w, x)


def swapped(value):
    return lax.ppermute(value, "side", [(0, 1), (1, 0)])


def padded(array, rows, columns):
    return jnp.pad(array, ((0, rows - array.shape[0]), (0, columns - array.shape[1])))


def local(
    right_side,
    couplings,
    channel_rates,
    weight_in,
    weight_mid,
    weight_out,
    inverse_cov,
    profile_cells,
    profile_counts,
    gate_first,
    gate_second,
):
    side = lax.axis_index("side")
    lats, lons, width = right_side.shape
    slots = profile_cells.shape[1]
    wide = -(-width // LANES) * LANES
    channels = -(-weight_out.shape[1] // LANES) * LANES
    latitude = lax.axis_index("row") * lats + jnp.arange(lats)
    north_open = (latitude < lats * lax.axis_size("row") - 1)[:, None]
    south_open = (latitude > 0)[:, None]
    weights = jnp.stack(
        [
            couplings[0],
            couplings[1],
            jnp.where(north_open, couplings[2], 0.0),
            jnp.where(south_open, couplings[3], 0.0),
        ],
        axis=2,
    )
    rates = channel_rates.reshape(1, width)
    halves = [lax.dynamic_slice_in_dim(weight_in, part * width, width, 0) for part in (side, 1 - side)]
    matrices = [padded(half, wide, half.shape[1]) for half in halves]
    matrices += [weight_mid, padded(weight_out, weight_out.shape[0], channels), padded(inverse_cov, channels, channels)]
    split_scratch = [pltpu.VMEM(matrix.shape, jnp.bfloat16) for matrix in matrices for _ in range(2)]
    lat_edge, lon_edge = (lons, width), (lats, width)

    def spread(field, edges, known, sums, is_first):
        around = halos(*edges)
        image = [pltpu.VMEM((lats * lons, wide), jnp.float32)]
        specs = [VMEM] * 7 + [SMEM] * 2
        operands = (field, *around, weights, rates, profile_cells, profile_counts)
        own, other = call(gather_kernel, [(slots, wide)] * 2, specs, image, *operands)
        other = swapped(other)
        operands = (own, other, gate_first, gate_second, *matrices, profile_counts)
        shapes = [(slots, wide)] * 2 + [(8, LANES)]
        own, other, scale = call(network_kernel, shapes, [VMEM] * 9 + [SMEM], split_scratch, *operands)
        other = swapped(other)
        shapes = [(lats * lons, wide), lat_edge, lat_edge, lon_edge, lon_edge]
        operands = (own, other, weights, rates, profile_cells, profile_counts)
        summed, *edges = call(scatter_kernel, shapes, [VMEM] * 4 + [SMEM] * 2, [], *operands)
        around = halos(*edges)
        shapes = [field.shape] + ([lat_edge, lat_edge, lon_edge, lon_edge] if is_first else []) + [(8, LANES)]
        operands = (summed, *around, weights, rates, known, sums)
        out, *edges, sums = call(functools.partial(adjoint_kernel, is_first), shapes, [VMEM] * 9, [], *operands)
        return out, edges, sums, scale

    edges = (right_side[0], right_side[lats - 1], right_side[:, 0], right_side[:, lons - 1])
    first, edges, sums, scale = spread(right_side, edges, right_side, jnp.zeros((8, LANES), jnp.float32), True)
    second, _, sums, _ = spread(first, edges, first, sums, False)
    return tuple(finish(all_sums(sums), scale, right_side, first, second))


def solution(mesh):
    in_specs = (
        P("row", "col", "side"),
        P(None, "row", "col"),
        P("side"),
        P(),
        P(),
        P(),
        P(),
        P(None, ("row", "col")),
        P(),
        P(("side", "row", "col"), None),
        P(("side", "row", "col"), None),
    )
    out_specs = (P("row", "col", "side"), P("row", "col", "side"))
    return jax.shard_map(local, mesh=mesh, in_specs=in_specs, out_specs=out_specs, check_vma=False)
```

```python
import functools

import jax
import jax.numpy as jnp
from jax import lax
from jax.experimental import pallas as pl
from jax.experimental.pallas import tpu as pltpu
from jax.sharding import PartitionSpec as P

MESH = pl.DeviceIdType.MESH


def sums_kernel(sides, rows, cols, x_ref, o_ref, plane, line, send_sem, recv_sem):
    side, row, col = lax.axis_index("side"), lax.axis_index("row"), lax.axis_index("col")
    near = [
        (lax.rem(side + ds, sides), lax.rem(row + dr, rows), col)
        for ds in range(sides)
        for dr in range(rows)
        if ds + dr
    ]
    far = [(side, row, lax.rem(col + dc, cols)) for dc in range(1, cols)]
    barrier = pltpu.get_barrier_semaphore()
    for peer in near + far:
        pl.semaphore_signal(barrier, inc=1, device_id=peer, device_id_type=MESH)
    pl.semaphore_wait(barrier, len(near) + len(far))

    def exchange(value, peers, buffer, slot, first):
        buffer[slot] = value
        copies = [
            pltpu.make_async_remote_copy(
                src_ref=buffer.at[slot],
                dst_ref=buffer.at[slot],
                send_sem=send_sem.at[first + k],
                recv_sem=recv_sem.at[first + k],
                device_id=peer,
                device_id_type=MESH,
            )
            for k, peer in enumerate(peers)
        ]
        for copy in copies:
            copy.start()
        for copy in copies:
            copy.wait()
        return jnp.sum(buffer[...], axis=0)

    plane_sum = exchange(x_ref[...], near, plane, side * rows + row, 0)
    o_ref[...] = exchange(plane_sum, far, line, col, len(near))


VMEM = pl.BlockSpec(memory_space=pltpu.VMEM)
SMEM = pl.BlockSpec(memory_space=pltpu.SMEM)
LANES = 128
MIB = 1024 * 1024


def call(kernel, grant, shapes, specs, scratch, *operands, **params):
    out = [jax.ShapeDtypeStruct(shape, jnp.float32) for shape in shapes]
    params = pltpu.CompilerParams(vmem_limit_bytes=grant * MIB, **params)
    return pl.pallas_call(
        kernel,
        out_shape=out,
        in_specs=specs,
        out_specs=[VMEM] * len(out),
        scratch_shapes=scratch,
        compiler_params=params,
    )(*operands)


def all_sums(block):
    sides, rows, cols = (lax.axis_size(axis) for axis in ("side", "row", "col"))
    count = sides * rows - 1 + cols - 1
    scratch = [
        pltpu.VMEM((sides * rows, *block.shape), jnp.float32),
        pltpu.VMEM((cols, *block.shape), jnp.float32),
        pltpu.SemaphoreType.DMA((count,)),
        pltpu.SemaphoreType.DMA((count,)),
    ]
    kernel = functools.partial(sums_kernel, sides, rows, cols)
    return call(kernel, 4, [block.shape], [VMEM], scratch, block, collective_id=0, has_side_effects=True)[0]


def halo_kernel(rows, cols, first_lat, last_lat, first_lon, last_lon, *rest):
    outs, lands, (send_sem, recv_sem) = rest[:4], rest[4:8], rest[8:]
    side, row, col = lax.axis_index("side"), lax.axis_index("row"), lax.axis_index("col")
    below = (side, lax.rem(row + rows - 1, rows), col)
    above = (side, lax.rem(row + 1, rows), col)
    behind = (side, row, lax.rem(col + cols - 1, cols))
    ahead = (side, row, lax.rem(col + 1, cols))
    peers = (above, below, ahead, behind)
    barrier = pltpu.get_barrier_semaphore()
    for peer in peers:
        pl.semaphore_signal(barrier, inc=1, device_id=peer, device_id_type=MESH)
    pl.semaphore_wait(barrier, 4)
    copies = [
        pltpu.make_async_remote_copy(
            src_ref=source,
            dst_ref=land,
            send_sem=send_sem.at[k],
            recv_sem=recv_sem.at[k],
            device_id=peer,
            device_id_type=MESH,
        )
        for k, (source, land, peer) in enumerate(zip((last_lat, first_lat, last_lon, first_lon), lands, peers))
    ]
    for copy in copies:
        copy.start()
    for copy, land, out in zip(copies, lands, outs):
        copy.wait()
        out[...] = land[...]


def halos(first_lat, last_lat, first_lon, last_lon):
    kernel = functools.partial(halo_kernel, lax.axis_size("row"), lax.axis_size("col"))
    shapes = [first_lat.shape, first_lat.shape, first_lon.shape, first_lon.shape]
    scratch = [pltpu.VMEM(shape, jnp.float32) for shape in shapes]
    scratch += [pltpu.SemaphoreType.DMA((4,)), pltpu.SemaphoreType.DMA((4,))]
    operands = (first_lat, last_lat, first_lon, last_lon)
    return call(kernel, 4, shapes, [VMEM] * 4, scratch, *operands, collective_id=1, has_side_effects=True)


def live_counts(counts):
    side = lax.axis_index("side")
    tiles = lax.axis_size("row") * lax.axis_size("col")
    tile = lax.axis_index("row") * lax.axis_size("col") + lax.axis_index("col")
    return (side, counts[side * tiles + tile]), (1 - side, counts[(1 - side) * tiles + tile])


def over_lines(lats, body, state):
    steps = (lats - 2) // 4

    def step(j, state):
        for k in range(4):
            state = body(1 + j * 4 + k, state)
        return state

    state = lax.fori_loop(0, steps, step, state)
    for i in range(1 + steps * 4, lats - 1):
        state = body(i, state)
    return state


def gather_kernel(field, before, after, left, right, weights, rates, cells, counts, own, other, image):
    lats, lons, width = field.shape
    rate = rates[...]
    whole = width // LANES * LANES
    image[:, whole:] = jnp.zeros((image.shape[0], image.shape[1] - whole), jnp.float32)

    def line(i, value, following, preceding):
        weight = weights[i]
        east = jnp.concatenate([value[1:], right[pl.ds(i, 1)]], axis=0)
        west = jnp.concatenate([left[pl.ds(i, 1)], value[:-1]], axis=0)
        flux = weight[:, 0:1] * (east - value) + weight[:, 1:2] * (west - value)
        flux = flux + weight[:, 2:3] * (following - value) + weight[:, 3:4] * (preceding - value)
        image[pl.ds(pl.multiple_of(i * lons, lons), lons), :width] = value + rate * flux

    line(0, field[0], field[1], before[...])
    line(lats - 1, field[lats - 1], after[...], field[lats - 2])

    def inner(i, state):
        line(i, field[i], field[i + 1], field[i - 1])
        return state

    over_lines(lats, inner, 0)

    for (side, live), out in zip(live_counts(counts), (own, other)):

        @pl.loop(0, (live + 15) // 16)
        def _(j):
            base = pl.multiple_of(j * 16, 16)
            lines = [image[pl.ds(cells[side, base + k], 1)] for k in range(16)]
            out[pl.ds(base, 16)] = jnp.concatenate(lines, axis=0)


def scatter_kernel(own, other, weights, rates, cells, counts, spread, to_before, to_after, to_left, to_right, *parts):
    lats, lons, _ = weights.shape
    width = rates.shape[1]
    rate = rates[...]
    for part in parts:
        part[...] = jnp.zeros_like(part)
    for (side, live), grads in zip(live_counts(counts), (own, other)):

        @pl.loop(0, (live + len(parts) - 1) // len(parts))
        def _(j):
            base = j * len(parts)
            places = [pl.ds(cells[side, base + k], 1) for k in range(len(parts))]
            sums = []
            for k, (part, place) in enumerate(zip(parts, places)):
                term = jnp.where(base + k < live, grads[pl.ds(base + k, 1)], 0.0)
                sums.append(part[place] + term)
            for part, place, total in zip(parts, places, sums):
                part[place] = total

    block = 8 * lons

    @pl.loop(0, spread.shape[0] // block)
    def _(j):
        lines = pl.ds(pl.multiple_of(j * block, block), block)
        spread[lines] = (parts[0][lines] + parts[1][lines]) + (parts[2][lines] + parts[3][lines])

    to_before[...] = weights[0][:, 3:4] * (rate * spread[:lons, :width])
    to_after[...] = weights[lats - 1][:, 2:3] * (rate * spread[(lats - 1) * lons :, :width])

    @pl.loop(0, lats // 8)
    def _(j):
        starts, ends = [], []
        for k in range(8):
            i = j * 8 + k
            base = pl.multiple_of(i * lons, lons)
            weight = weights[i]
            starts.append(weight[:1, 1:2] * (rate * spread[pl.ds(base, 1), :width]))
            ends.append(weight[lons - 1 :, 0:1] * (rate * spread[pl.ds(base + lons - 1, 1), :width]))
        lines = pl.ds(pl.multiple_of(j * 8, 8), 8)
        to_left[lines] = jnp.concatenate(starts, axis=0)
        to_right[lines] = jnp.concatenate(ends, axis=0)


def adjoint_kernel(is_first, spread, before, after, left, right, weights, rates, field, sums, out, *rest):
    lats, lons, width = field.shape
    rate = rates[...]

    def scaled(i):
        return rate * spread[pl.ds(pl.multiple_of(i * lons, lons), lons), :width]

    def line(i, preceding, following, totals):
        weight = weights[i]
        value = spread[pl.ds(pl.multiple_of(i * lons, lons), lons), :width]
        flow = rate * value
        east = weight[:, 0:1] * flow
        west = weight[:, 1:2] * flow
        total = weight[:, 0:1] + weight[:, 1:2] + weight[:, 2:3] + weight[:, 3:4]
        result = value - total * flow + preceding + following
        result = result + jnp.concatenate([left[pl.ds(i, 1)], east[:-1]], axis=0)
        result = result + jnp.concatenate([west[1:], right[pl.ds(i, 1)]], axis=0)
        out[i] = result
        known = field[i]
        if not is_first:
            return (totals[0] + known * result,)
        rest[2][pl.ds(i, 1)] = result[:1]
        rest[3][pl.ds(i, 1)] = result[lons - 1 :]
        return totals[0] + known * known, totals[1] + known * result, totals[2] + result * result

    def inner(i, totals):
        return line(i, weights[i - 1][:, 2:3] * scaled(i - 1), weights[i + 1][:, 3:4] * scaled(i + 1), totals)

    totals = tuple(jnp.zeros((lons, width), jnp.float32) for _ in range(3 if is_first else 1))
    totals = line(0, before[...], weights[1][:, 3:4] * scaled(1), totals)
    totals = over_lines(lats, inner, totals)
    totals = line(lats - 1, weights[lats - 2][:, 2:3] * scaled(lats - 2), after[...], totals)
    lines = lax.broadcasted_iota(jnp.int32, sums.shape, 0)
    block = sums[...]
    for k, total in enumerate(totals):
        block = jnp.where(lines == (k if is_first else 3), jnp.sum(total), block)
    if is_first:
        rest[0][...] = out[0]
        rest[1][...] = out[lats - 1]
    rest[-1][...] = block


def network_kernel(own, other, gate_one, gate_two, w_own, w_other, w_mid, w_out, cov, counts, d_own, d_other, scale_out, *scratch):
    pairs = [scratch[2 * k : 2 * k + 2] for k in range(5)]
    squares = []
    for full, (high, low) in zip((w_own, w_other, w_mid, w_out, cov), pairs):
        chunk = 32
        rows, columns = full.shape

        def store(start, value, high=high, low=low, columns=columns):
            lines = pl.ds(start, chunk)
            rounded = value.astype(jnp.bfloat16)
            high[lines, :columns] = rounded
            low[lines, :columns] = (value - rounded.astype(jnp.float32)).astype(jnp.bfloat16)
            return value * value

        def split(c, total, full=full, store=store):
            start = pl.multiple_of(c * chunk, chunk)
            return total + store(start, full[pl.ds(start, chunk)])

        if high.shape != full.shape:
            high[...] = jnp.zeros_like(high)
            low[...] = jnp.zeros_like(low)
        total = lax.fori_loop(0, rows // chunk, split, jnp.zeros((chunk, columns), jnp.float32))
        left = rows % chunk
        if left:
            rest = jnp.concatenate([full[rows - left :], jnp.zeros((chunk - left, columns), jnp.float32)], axis=0)
            total = total + store(rows - left, rest)
        squares.append(jnp.sum(total, axis=(0, 1), keepdims=True))
    bound = (squares[0] + squares[1]) * squares[2] * squares[3] * jnp.sqrt(squares[4])
    scale = 1.0 / jnp.maximum(bound, 1.0)
    scale_out[...] = jnp.broadcast_to(scale, scale_out.shape)
    p_own, p_other, p_mid, p_out, p_cov = pairs

    def product(value, pair, back=False):
        dims = (((1,), (1 if back else 0,)), ((), ()))
        high = value.astype(jnp.bfloat16)
        low = (value - high.astype(jnp.float32)).astype(jnp.bfloat16)

        def dot(left, right):
            return lax.dot_general(left, right[...], dims, preferred_element_type=jnp.float32)

        return dot(high, pair[0]) + (dot(low, pair[0]) + dot(high, pair[1]))

    rows = min(256, own.shape[0])
    live = live_counts(counts)[0][1]

    @pl.loop(0, (live + rows - 1) // rows)
    def _(j):
        lines = pl.ds(pl.multiple_of(j * rows, rows), rows)
        g1 = gate_one[lines].astype(jnp.float32)
        hidden = (product(own[lines], p_own) + product(other[lines], p_other)) * g1
        hidden = product(hidden, p_mid) * gate_two[lines].astype(jnp.float32)
        weighted = product(product(hidden, p_out, True), p_cov) * scale
        back = product(weighted, p_out) * gate_two[lines].astype(jnp.float32)
        back = product(back, p_mid, True) * gate_one[lines].astype(jnp.float32)
        d_own[lines] = product(back, p_own, True)
        d_other[lines] = product(back, p_other, True)


def combination(scale, bb, bw, ww, wx):
    bw = bw / scale
    curve = bb + bw
    step = bb / curve
    rest = bw / curve
    grown = step / scale
    ratio = (grown * ww / bb) * grown - rest * rest
    norm = ratio * bb
    along = norm + rest * rest * bw - 2.0 * rest * (grown * ww / scale) + grown * (grown * wx) / scale
    second = norm / (along - ratio * norm / step)
    mixed = rest + ratio
    of_solution = (step + second * mixed, -second * grown)
    of_residual = (
        rest - second * mixed,
        -grown - second * (mixed / scale - grown),
        (second / scale) * grown,
    )
    return of_solution, of_residual


def finish_kernel(sums, scale, b, w, x, solution, residual):
    values = [sums[k : k + 1, 0:1] for k in range(4)]
    of_solution, of_residual = combination(scale[0:1, 0:1], *values)
    solution[...] = of_solution[0] * b[...] + of_solution[1] * w[...]
    residual[...] = of_residual[0] * b[...] + of_residual[1] * w[...] + of_residual[2] * x[...]


def finish(sums, scale, b, w, x):
    lats, lons, width = b.shape
    part = 8 if lats % 8 == 0 else lats
    whole = pl.BlockSpec(sums.shape, lambda i: (0, 0))
    block = pl.BlockSpec((part, lons, width), lambda i: (i, 0, 0))
    return pl.pallas_call(
        finish_kernel,
        grid=(lats // part,),
        out_shape=[jax.ShapeDtypeStruct(b.shape, jnp.float32)] * 2,
        in_specs=[whole, whole, block, block, block],
        out_specs=[block, block],
        compiler_params=pltpu.CompilerParams(vmem_limit_bytes=24 * MIB),
    )(sums, scale, b, w, x)


def swapped(value):
    return lax.ppermute(value, "side", [(0, 1), (1, 0)])


def local(
    right_side,
    couplings,
    channel_rates,
    weight_in,
    weight_mid,
    weight_out,
    inverse_cov,
    profile_cells,
    profile_counts,
    gate_first,
    gate_second,
):
    side = lax.axis_index("side")
    lats, lons, width = right_side.shape
    slots = profile_cells.shape[1]
    wide = -(-width // LANES) * LANES
    channels = -(-weight_out.shape[1] // LANES) * LANES
    latitude = lax.axis_index("row") * lats + jnp.arange(lats)
    north_open = (latitude < lats * lax.axis_size("row") - 1)[:, None]
    south_open = (latitude > 0)[:, None]
    weights = jnp.stack(
        [
            couplings[0],
            couplings[1],
            jnp.where(north_open, couplings[2], 0.0),
            jnp.where(south_open, couplings[3], 0.0),
        ],
        axis=2,
    )
    rates = channel_rates.reshape(1, width)
    halves = [lax.dynamic_slice_in_dim(weight_in, part * width, width, 0) for part in (side, 1 - side)]
    hidden = weight_in.shape[1]
    matrices = [*halves, weight_mid, weight_out.T, inverse_cov]
    shapes = [(wide, hidden), (wide, hidden), (hidden, hidden), (channels, hidden), (channels, channels)]
    split_scratch = [pltpu.VMEM(shape, jnp.bfloat16) for shape in shapes for _ in range(2)]
    lat_edge, lon_edge = (lons, width), (lats, width)

    def spread(field, edges, known, sums, is_first):
        around = halos(*edges)
        image = [pltpu.VMEM((lats * lons, wide), jnp.float32)]
        specs = [VMEM] * 7 + [SMEM] * 2
        operands = (field, *around, weights, rates, profile_cells, profile_counts)
        own, other = call(gather_kernel, 16, [(slots, wide)] * 2, specs, image, *operands)
        other = swapped(other)
        operands = (own, other, gate_first, gate_second, *matrices, profile_counts)
        shapes = [(slots, wide)] * 2 + [(8, LANES)]
        own, other, scale = call(network_kernel, 46, shapes, [VMEM] * 9 + [SMEM], split_scratch, *operands)
        other = swapped(other)
        parts = [pltpu.VMEM((lats * lons, wide), jnp.float32)] * 4
        shapes = [(lats * lons, wide), lat_edge, lat_edge, lon_edge, lon_edge]
        operands = (own, other, weights, rates, profile_cells, profile_counts)
        summed, *edges = call(scatter_kernel, 24, shapes, [VMEM] * 4 + [SMEM] * 2, parts, *operands)
        around = halos(*edges)
        shapes = [field.shape] + ([lat_edge, lat_edge, lon_edge, lon_edge] if is_first else []) + [(8, LANES)]
        operands = (summed, *around, weights, rates, known, sums)
        out, *edges, sums = call(functools.partial(adjoint_kernel, is_first), 16, shapes, [VMEM] * 9, [], *operands)
        return out, edges, sums, scale

    edges = (right_side[0], right_side[lats - 1], right_side[:, 0], right_side[:, lons - 1])
    first, edges, sums, scale = spread(right_side, edges, right_side, jnp.zeros((8, LANES), jnp.float32), True)
    second, _, sums, _ = spread(first, edges, first, sums, False)
    return tuple(finish(all_sums(sums), scale, right_side, first, second))


def solution(mesh):
    in_specs = (
        P("row", "col", "side"),
        P(None, "row", "col"),
        P("side"),
        P(),
        P(),
        P(),
        P(),
        P(None, ("row", "col")),
        P(),
        P(("side", "row", "col"), None),
        P(("side", "row", "col"), None),
    )
    out_specs = (P("row", "col", "side"), P("row", "col", "side"))
    return jax.shard_map(local, mesh=mesh, in_specs=in_specs, out_specs=out_specs, check_vma=False)
```

```python
import functools

import jax
import jax.numpy as jnp
from jax import lax
from jax.experimental import pallas as pl
from jax.experimental.pallas import tpu as pltpu
from jax.sharding import PartitionSpec as P

MESH = pl.DeviceIdType.MESH


def sums_kernel(sides, rows, cols, x_ref, o_ref, plane, line, send_sem, recv_sem):
    side, row, col = lax.axis_index("side"), lax.axis_index("row"), lax.axis_index("col")
    near = [
        (lax.rem(side + ds, sides), lax.rem(row + dr, rows), col)
        for ds in range(sides)
        for dr in range(rows)
        if ds + dr
    ]
    far = [(side, row, lax.rem(col + dc, cols)) for dc in range(1, cols)]
    barrier = pltpu.get_barrier_semaphore()
    for peer in near + far:
        pl.semaphore_signal(barrier, inc=1, device_id=peer, device_id_type=MESH)
    pl.semaphore_wait(barrier, len(near) + len(far))

    def exchange(value, peers, buffer, slot, first):
        buffer[slot] = value
        copies = [
            pltpu.make_async_remote_copy(
                src_ref=buffer.at[slot],
                dst_ref=buffer.at[slot],
                send_sem=send_sem.at[first + k],
                recv_sem=recv_sem.at[first + k],
                device_id=peer,
                device_id_type=MESH,
            )
            for k, peer in enumerate(peers)
        ]
        for copy in copies:
            copy.start()
        for copy in copies:
            copy.wait()
        return jnp.sum(buffer[...], axis=0)

    plane_sum = exchange(x_ref[...], near, plane, side * rows + row, 0)
    o_ref[...] = exchange(plane_sum, far, line, col, len(near))


VMEM = pl.BlockSpec(memory_space=pltpu.VMEM)
SMEM = pl.BlockSpec(memory_space=pltpu.SMEM)
LANES = 128
MIB = 1024 * 1024


def call(kernel, grant, shapes, specs, scratch, *operands, **params):
    out = [jax.ShapeDtypeStruct(shape[:2] if shape[-1] == "half" else shape, jnp.bfloat16 if shape[-1] == "half" else jnp.float32) for shape in shapes]
    params = pltpu.CompilerParams(vmem_limit_bytes=grant * MIB, **params)
    return pl.pallas_call(
        kernel,
        out_shape=out,
        in_specs=specs,
        out_specs=[VMEM] * len(out),
        scratch_shapes=scratch,
        compiler_params=params,
    )(*operands)


def all_sums(block):
    sides, rows, cols = (lax.axis_size(axis) for axis in ("side", "row", "col"))
    count = sides * rows - 1 + cols - 1
    scratch = [
        pltpu.VMEM((sides * rows, *block.shape), jnp.float32),
        pltpu.VMEM((cols, *block.shape), jnp.float32),
        pltpu.SemaphoreType.DMA((count,)),
        pltpu.SemaphoreType.DMA((count,)),
    ]
    kernel = functools.partial(sums_kernel, sides, rows, cols)
    return call(kernel, 4, [block.shape], [VMEM], scratch, block, collective_id=0, has_side_effects=True)[0]


def halo_kernel(rows, cols, first_lat, last_lat, first_lon, last_lon, *rest):
    outs, lands, (send_sem, recv_sem) = rest[:4], rest[4:8], rest[8:]
    side, row, col = lax.axis_index("side"), lax.axis_index("row"), lax.axis_index("col")
    below = (side, lax.rem(row + rows - 1, rows), col)
    above = (side, lax.rem(row + 1, rows), col)
    behind = (side, row, lax.rem(col + cols - 1, cols))
    ahead = (side, row, lax.rem(col + 1, cols))
    peers = (above, below, ahead, behind)
    barrier = pltpu.get_barrier_semaphore()
    for peer in peers:
        pl.semaphore_signal(barrier, inc=1, device_id=peer, device_id_type=MESH)
    pl.semaphore_wait(barrier, 4)
    copies = [
        pltpu.make_async_remote_copy(
            src_ref=source,
            dst_ref=land,
            send_sem=send_sem.at[k],
            recv_sem=recv_sem.at[k],
            device_id=peer,
            device_id_type=MESH,
        )
        for k, (source, land, peer) in enumerate(zip((last_lat, first_lat, last_lon, first_lon), lands, peers))
    ]
    for copy in copies:
        copy.start()
    for copy, land, out in zip(copies, lands, outs):
        copy.wait()
        out[...] = land[...]


def halos(first_lat, last_lat, first_lon, last_lon):
    kernel = functools.partial(halo_kernel, lax.axis_size("row"), lax.axis_size("col"))
    shapes = [first_lat.shape, first_lat.shape, first_lon.shape, first_lon.shape]
    scratch = [pltpu.VMEM(shape, jnp.float32) for shape in shapes]
    scratch += [pltpu.SemaphoreType.DMA((4,)), pltpu.SemaphoreType.DMA((4,))]
    operands = (first_lat, last_lat, first_lon, last_lon)
    return call(kernel, 4, shapes, [VMEM] * 4, scratch, *operands, collective_id=1, has_side_effects=True)


def live_counts(counts):
    side = lax.axis_index("side")
    tiles = lax.axis_size("row") * lax.axis_size("col")
    tile = lax.axis_index("row") * lax.axis_size("col") + lax.axis_index("col")
    return (side, counts[side * tiles + tile]), (1 - side, counts[(1 - side) * tiles + tile])


def over_lines(lats, body, state):
    steps = (lats - 2) // 4

    def step(j, state):
        for k in range(4):
            state = body(1 + j * 4 + k, state)
        return state

    state = lax.fori_loop(0, steps, step, state)
    for i in range(1 + steps * 4, lats - 1):
        state = body(i, state)
    return state


def gather_kernel(field, before, after, left, right, weights, rates, cells, counts, own, other, image):
    lats, lons, width = field.shape
    rate = rates[...]
    whole = width // LANES * LANES
    image[:, whole:] = jnp.zeros((image.shape[0], image.shape[1] - whole), jnp.float32)

    def line(i, value, following, preceding):
        weight = weights[i]
        east = jnp.concatenate([value[1:], right[pl.ds(i, 1)]], axis=0)
        west = jnp.concatenate([left[pl.ds(i, 1)], value[:-1]], axis=0)
        flux = weight[:, 0:1] * (east - value) + weight[:, 1:2] * (west - value)
        flux = flux + weight[:, 2:3] * (following - value) + weight[:, 3:4] * (preceding - value)
        image[pl.ds(pl.multiple_of(i * lons, lons), lons), :width] = value + rate * flux

    line(0, field[0], field[1], before[...])
    line(lats - 1, field[lats - 1], after[...], field[lats - 2])

    def inner(i, state):
        line(i, field[i], field[i + 1], field[i - 1])
        return state

    over_lines(lats, inner, 0)

    for (side, live), out in zip(live_counts(counts), (own, other)):

        @pl.loop(0, (live + 15) // 16)
        def _(j):
            base = pl.multiple_of(j * 16, 16)
            lines = [image[pl.ds(cells[side, base + k], 1)] for k in range(16)]
            out[pl.ds(base, 16)] = jnp.concatenate(lines, axis=0)


def scatter_kernel(own, other, weights, rates, cells, counts, spread, to_before, to_after, to_left, to_right, *parts):
    lats, lons, _ = weights.shape
    width = rates.shape[1]
    rate = rates[...]
    for part in parts:
        part[...] = jnp.zeros_like(part)
    for (side, live), grads in zip(live_counts(counts), (own, other)):

        @pl.loop(0, (live + len(parts) - 1) // len(parts))
        def _(j):
            base = j * len(parts)
            places = [pl.ds(cells[side, base + k], 1) for k in range(len(parts))]
            sums = []
            for k, (part, place) in enumerate(zip(parts, places)):
                term = jnp.where(base + k < live, grads[pl.ds(base + k, 1)], 0.0)
                sums.append(part[place] + term)
            for part, place, total in zip(parts, places, sums):
                part[place] = total

    block = 8 * lons

    @pl.loop(0, spread.shape[0] // block)
    def _(j):
        lines = pl.ds(pl.multiple_of(j * block, block), block)
        spread[lines] = (parts[0][lines] + parts[1][lines]) + (parts[2][lines] + parts[3][lines])

    to_before[...] = weights[0][:, 3:4] * (rate * spread[:lons, :width])
    to_after[...] = weights[lats - 1][:, 2:3] * (rate * spread[(lats - 1) * lons :, :width])

    @pl.loop(0, lats // 8)
    def _(j):
        starts, ends = [], []
        for k in range(8):
            i = j * 8 + k
            base = pl.multiple_of(i * lons, lons)
            weight = weights[i]
            starts.append(weight[:1, 1:2] * (rate * spread[pl.ds(base, 1), :width]))
            ends.append(weight[lons - 1 :, 0:1] * (rate * spread[pl.ds(base + lons - 1, 1), :width]))
        lines = pl.ds(pl.multiple_of(j * 8, 8), 8)
        to_left[lines] = jnp.concatenate(starts, axis=0)
        to_right[lines] = jnp.concatenate(ends, axis=0)


def adjoint_kernel(is_first, spread, before, after, left, right, weights, rates, field, sums, out, *rest):
    lats, lons, width = field.shape
    rate = rates[...]

    def scaled(i):
        return rate * spread[pl.ds(pl.multiple_of(i * lons, lons), lons), :width]

    def line(i, preceding, following, totals):
        weight = weights[i]
        value = spread[pl.ds(pl.multiple_of(i * lons, lons), lons), :width]
        flow = rate * value
        east = weight[:, 0:1] * flow
        west = weight[:, 1:2] * flow
        total = weight[:, 0:1] + weight[:, 1:2] + weight[:, 2:3] + weight[:, 3:4]
        result = value - total * flow + preceding + following
        result = result + jnp.concatenate([left[pl.ds(i, 1)], east[:-1]], axis=0)
        result = result + jnp.concatenate([west[1:], right[pl.ds(i, 1)]], axis=0)
        out[i] = result
        known = field[i]
        if not is_first:
            return (totals[0] + known * result,)
        rest[2][pl.ds(i, 1)] = result[:1]
        rest[3][pl.ds(i, 1)] = result[lons - 1 :]
        return totals[0] + known * known, totals[1] + known * result, totals[2] + result * result

    def inner(i, totals):
        return line(i, weights[i - 1][:, 2:3] * scaled(i - 1), weights[i + 1][:, 3:4] * scaled(i + 1), totals)

    totals = tuple(jnp.zeros((lons, width), jnp.float32) for _ in range(3 if is_first else 1))
    totals = line(0, before[...], weights[1][:, 3:4] * scaled(1), totals)
    totals = over_lines(lats, inner, totals)
    totals = line(lats - 1, weights[lats - 2][:, 2:3] * scaled(lats - 2), after[...], totals)
    lines = lax.broadcasted_iota(jnp.int32, sums.shape, 0)
    block = sums[...]
    for k, total in enumerate(totals):
        block = jnp.where(lines == (k if is_first else 3), jnp.sum(total), block)
    if is_first:
        rest[0][...] = out[0]
        rest[1][...] = out[lats - 1]
    rest[-1][...] = block


def split_kernel(wide, w_own, w_other, w_mid, w_out, cov, *outs):
    pairs = [outs[2 * k : 2 * k + 2] for k in range(4)]
    scale_out = outs[8]
    for pair in (pairs[0], pairs[2], pairs[3]):
        for half in pair:
            half[...] = jnp.zeros_like(half)
    chunk = 32

    def squares(full, pair, base):
        high, low = pair
        rows, columns = full.shape

        def store(start, value):
            lines = pl.ds(start, chunk)
            rounded = value.astype(jnp.bfloat16)
            high[lines, :columns] = rounded
            low[lines, :columns] = (value - rounded.astype(jnp.float32)).astype(jnp.bfloat16)
            square = value * value
            return (square[:8] + square[8:16]) + (square[16:24] + square[24:])

        def split(c, total):
            start = pl.multiple_of(c * chunk, chunk)
            return total + store(pl.multiple_of(base + start, chunk), full[pl.ds(start, chunk)])

        total = lax.fori_loop(0, rows // chunk, split, jnp.zeros((8, columns), jnp.float32))
        left = rows % chunk
        if left:
            rest = jnp.concatenate([full[rows - left :], jnp.zeros((chunk - left, columns), jnp.float32)], axis=0)
            total = total + store(base + rows - left, rest)
        return jnp.sum(total, axis=(0, 1), keepdims=True)

    first = squares(w_own, pairs[0], 0) + squares(w_other, pairs[0], wide)
    bound = first * squares(w_mid, pairs[1], 0) * squares(w_out, pairs[2], 0)
    scale = 1.0 / jnp.maximum(bound * jnp.sqrt(squares(cov, pairs[3], 0)), 1.0)
    scale_out[...] = jnp.broadcast_to(scale, scale_out.shape)


def network_kernel(own, other, gate_one, gate_two, *rest):
    p_in, p_mid, p_out, p_cov = (rest[2 * k : 2 * k + 2] for k in range(4))
    scale, counts, d_own, d_other = rest[8:]
    factor = scale[0:1, 0:1]
    wide = own.shape[1]

    def product(value, pair, back=False):
        dims = (((1,), (1 if back else 0,)), ((), ()))
        high = value.astype(jnp.bfloat16)
        low = (value - high.astype(jnp.float32)).astype(jnp.bfloat16)

        def dot(left, right):
            return lax.dot_general(left, right[...], dims, preferred_element_type=jnp.float32)

        return dot(high, pair[0]) + (dot(low, pair[0]) + dot(high, pair[1]))

    rows = min(256, own.shape[0])
    live = live_counts(counts)[0][1]

    @pl.loop(0, (live + rows - 1) // rows)
    def _(j):
        lines = pl.ds(pl.multiple_of(j * rows, rows), rows)
        columns = jnp.concatenate([own[lines], other[lines]], axis=1)
        hidden = product(columns, p_in) * gate_one[lines].astype(jnp.float32)
        hidden = product(hidden, p_mid) * gate_two[lines].astype(jnp.float32)
        weighted = product(product(hidden, p_out, True), p_cov) * factor
        back = product(weighted, p_out) * gate_two[lines].astype(jnp.float32)
        back = product(back, p_mid, True) * gate_one[lines].astype(jnp.float32)
        terms = product(back, p_in, True)
        d_own[lines] = terms[:, :wide]
        d_other[lines] = terms[:, wide:]


def combination(scale, bb, bw, ww, wx):
    bw = bw / scale
    curve = bb + bw
    step = bb / curve
    rest = bw / curve
    grown = step / scale
    ratio = (grown * ww / bb) * grown - rest * rest
    norm = ratio * bb
    along = norm + rest * rest * bw - 2.0 * rest * (grown * ww / scale) + grown * (grown * wx) / scale
    second = norm / (along - ratio * norm / step)
    mixed = rest + ratio
    of_solution = (step + second * mixed, -second * grown)
    of_residual = (
        rest - second * mixed,
        -grown - second * (mixed / scale - grown),
        (second / scale) * grown,
    )
    return of_solution, of_residual


def finish_kernel(sums, scale, b, w, x, solution, residual):
    values = [sums[k : k + 1, 0:1] for k in range(4)]
    of_solution, of_residual = combination(scale[0:1, 0:1], *values)
    solution[...] = of_solution[0] * b[...] + of_solution[1] * w[...]
    residual[...] = of_residual[0] * b[...] + of_residual[1] * w[...] + of_residual[2] * x[...]


def finish(sums, scale, b, w, x):
    lats, lons, width = b.shape
    part = 8 if lats % 8 == 0 else lats
    whole = pl.BlockSpec(sums.shape, lambda i: (0, 0))
    block = pl.BlockSpec((part, lons, width), lambda i: (i, 0, 0))
    return pl.pallas_call(
        finish_kernel,
        grid=(lats // part,),
        out_shape=[jax.ShapeDtypeStruct(b.shape, jnp.float32)] * 2,
        in_specs=[whole, whole, block, block, block],
        out_specs=[block, block],
        compiler_params=pltpu.CompilerParams(vmem_limit_bytes=24 * MIB),
    )(sums, scale, b, w, x)


def swapped(value):
    return lax.ppermute(value, "side", [(0, 1), (1, 0)])


def local(
    right_side,
    couplings,
    channel_rates,
    weight_in,
    weight_mid,
    weight_out,
    inverse_cov,
    profile_cells,
    profile_counts,
    gate_first,
    gate_second,
):
    side = lax.axis_index("side")
    lats, lons, width = right_side.shape
    slots = profile_cells.shape[1]
    wide = -(-width // LANES) * LANES
    channels = -(-weight_out.shape[1] // LANES) * LANES
    latitude = lax.axis_index("row") * lats + jnp.arange(lats)
    north_open = (latitude < lats * lax.axis_size("row") - 1)[:, None]
    south_open = (latitude > 0)[:, None]
    weights = jnp.stack(
        [
            couplings[0],
            couplings[1],
            jnp.where(north_open, couplings[2], 0.0),
            jnp.where(south_open, couplings[3], 0.0),
        ],
        axis=2,
    )
    rates = channel_rates.reshape(1, width)
    halves = [lax.dynamic_slice_in_dim(weight_in, part * width, width, 0) for part in (side, 1 - side)]
    hidden = weight_in.shape[1]
    hidden = weight_in.shape[1]
    matrices = (*halves, weight_mid, weight_out.T, inverse_cov)
    shapes = [(2 * wide, hidden), (hidden, hidden), (channels, hidden), (channels, channels)]
    shapes = [(*shape, "half") for shape in shapes for _ in range(2)] + [(8, LANES)]
    *pairs, scale = call(functools.partial(split_kernel, wide), 28, shapes, [VMEM] * 5, [], *matrices)
    lat_edge, lon_edge = (lons, width), (lats, width)

    def spread(field, edges, known, sums, is_first):
        around = halos(*edges)
        image = [pltpu.VMEM((lats * lons, wide), jnp.float32)]
        specs = [VMEM] * 7 + [SMEM] * 2
        operands = (field, *around, weights, rates, profile_cells, profile_counts)
        own, other = call(gather_kernel, 16, [(slots, wide)] * 2, specs, image, *operands)
        other = swapped(other)
        operands = (own, other, gate_first, gate_second, *pairs, scale, profile_counts)
        own, other = call(network_kernel, 36, [(slots, wide)] * 2, [VMEM] * 13 + [SMEM], [], *operands)
        other = swapped(other)
        parts = [pltpu.VMEM((lats * lons, wide), jnp.float32)] * 4
        shapes = [(lats * lons, wide), lat_edge, lat_edge, lon_edge, lon_edge]
        operands = (own, other, weights, rates, profile_cells, profile_counts)
        summed, *edges = call(scatter_kernel, 24, shapes, [VMEM] * 4 + [SMEM] * 2, parts, *operands)
        around = halos(*edges)
        shapes = [field.shape] + ([lat_edge, lat_edge, lon_edge, lon_edge] if is_first else []) + [(8, LANES)]
        operands = (summed, *around, weights, rates, known, sums)
        out, *edges, sums = call(functools.partial(adjoint_kernel, is_first), 16, shapes, [VMEM] * 9, [], *operands)
        return out, edges, sums

    edges = (right_side[0], right_side[lats - 1], right_side[:, 0], right_side[:, lons - 1])
    first, edges, sums = spread(right_side, edges, right_side, jnp.zeros((8, LANES), jnp.float32), True)
    second, _, sums = spread(first, edges, first, sums, False)
    return tuple(finish(all_sums(sums), scale, right_side, first, second))


def solution(mesh):
    in_specs = (
        P("row", "col", "side"),
        P(None, "row", "col"),
        P("side"),
        P(),
        P(),
        P(),
        P(),
        P(None, ("row", "col")),
        P(),
        P(("side", "row", "col"), None),
        P(("side", "row", "col"), None),
    )
    out_specs = (P("row", "col", "side"), P("row", "col", "side"))
    return jax.shard_map(local, mesh=mesh, in_specs=in_specs, out_specs=out_specs, check_vma=False)
```

```python
import functools

import jax
import jax.numpy as jnp
from jax import lax
from jax.experimental import pallas as pl
from jax.experimental.pallas import tpu as pltpu
from jax.sharding import PartitionSpec as P

MESH = pl.DeviceIdType.MESH


def sums_kernel(sides, rows, cols, x_ref, o_ref, plane, line, send_sem, recv_sem):
    side, row, col = lax.axis_index("side"), lax.axis_index("row"), lax.axis_index("col")
    near = [
        (lax.rem(side + ds, sides), lax.rem(row + dr, rows), col)
        for ds in range(sides)
        for dr in range(rows)
        if ds + dr
    ]
    far = [(side, row, lax.rem(col + dc, cols)) for dc in range(1, cols)]
    barrier = pltpu.get_barrier_semaphore()
    for peer in near + far:
        pl.semaphore_signal(barrier, inc=1, device_id=peer, device_id_type=MESH)
    pl.semaphore_wait(barrier, len(near) + len(far))

    def exchange(value, peers, buffer, slot, first):
        buffer[slot] = value
        copies = [
            pltpu.make_async_remote_copy(
                src_ref=buffer.at[slot],
                dst_ref=buffer.at[slot],
                send_sem=send_sem.at[first + k],
                recv_sem=recv_sem.at[first + k],
                device_id=peer,
                device_id_type=MESH,
            )
            for k, peer in enumerate(peers)
        ]
        for copy in copies:
            copy.start()
        for copy in copies:
            copy.wait()
        return jnp.sum(buffer[...], axis=0)

    plane_sum = exchange(x_ref[...], near, plane, side * rows + row, 0)
    o_ref[...] = exchange(plane_sum, far, line, col, len(near))


VMEM = pl.BlockSpec(memory_space=pltpu.VMEM)
SMEM = pl.BlockSpec(memory_space=pltpu.SMEM)
LANES = 128
MIB = 1024 * 1024


def call(kernel, grant, shapes, specs, scratch, *operands, **params):
    out = [jax.ShapeDtypeStruct(shape[:2] if shape[-1] == "half" else shape, jnp.bfloat16 if shape[-1] == "half" else jnp.float32) for shape in shapes]
    params = pltpu.CompilerParams(vmem_limit_bytes=grant * MIB, **params)
    return pl.pallas_call(
        kernel,
        out_shape=out,
        in_specs=specs,
        out_specs=[VMEM] * len(out),
        scratch_shapes=scratch,
        compiler_params=params,
    )(*operands)


def all_sums(block):
    sides, rows, cols = (lax.axis_size(axis) for axis in ("side", "row", "col"))
    count = sides * rows - 1 + cols - 1
    scratch = [
        pltpu.VMEM((sides * rows, *block.shape), jnp.float32),
        pltpu.VMEM((cols, *block.shape), jnp.float32),
        pltpu.SemaphoreType.DMA((count,)),
        pltpu.SemaphoreType.DMA((count,)),
    ]
    kernel = functools.partial(sums_kernel, sides, rows, cols)
    return call(kernel, 4, [block.shape], [VMEM], scratch, block, collective_id=0, has_side_effects=True)[0]


def halo_kernel(rows, cols, first_lat, last_lat, first_lon, last_lon, *rest):
    outs, lands, (send_sem, recv_sem) = rest[:4], rest[4:8], rest[8:]
    side, row, col = lax.axis_index("side"), lax.axis_index("row"), lax.axis_index("col")
    below = (side, lax.rem(row + rows - 1, rows), col)
    above = (side, lax.rem(row + 1, rows), col)
    behind = (side, row, lax.rem(col + cols - 1, cols))
    ahead = (side, row, lax.rem(col + 1, cols))
    peers = (above, below, ahead, behind)
    barrier = pltpu.get_barrier_semaphore()
    for peer in peers:
        pl.semaphore_signal(barrier, inc=1, device_id=peer, device_id_type=MESH)
    pl.semaphore_wait(barrier, 4)
    copies = [
        pltpu.make_async_remote_copy(
            src_ref=source,
            dst_ref=land,
            send_sem=send_sem.at[k],
            recv_sem=recv_sem.at[k],
            device_id=peer,
            device_id_type=MESH,
        )
        for k, (source, land, peer) in enumerate(zip((last_lat, first_lat, last_lon, first_lon), lands, peers))
    ]
    for copy in copies:
        copy.start()
    for copy, land, out in zip(copies, lands, outs):
        copy.wait()
        out[...] = land[...]


def halos(first_lat, last_lat, first_lon, last_lon):
    kernel = functools.partial(halo_kernel, lax.axis_size("row"), lax.axis_size("col"))
    shapes = [first_lat.shape, first_lat.shape, first_lon.shape, first_lon.shape]
    scratch = [pltpu.VMEM(shape, jnp.float32) for shape in shapes]
    scratch += [pltpu.SemaphoreType.DMA((4,)), pltpu.SemaphoreType.DMA((4,))]
    operands = (first_lat, last_lat, first_lon, last_lon)
    return call(kernel, 4, shapes, [VMEM] * 4, scratch, *operands, collective_id=1, has_side_effects=True)


def live_counts(counts):
    side = lax.axis_index("side")
    tiles = lax.axis_size("row") * lax.axis_size("col")
    tile = lax.axis_index("row") * lax.axis_size("col") + lax.axis_index("col")
    return (side, counts[side * tiles + tile]), (1 - side, counts[(1 - side) * tiles + tile])


def over_lines(lats, body, state):
    steps = (lats - 2) // 4

    def step(j, state):
        for k in range(4):
            state = body(1 + j * 4 + k, state)
        return state

    state = lax.fori_loop(0, steps, step, state)
    for i in range(1 + steps * 4, lats - 1):
        state = body(i, state)
    return state


def gather_kernel(field, before, after, left, right, weights, rates, cells, counts, own, other, image):
    lats, lons, width = field.shape
    rate = rates[...]
    whole = width // LANES * LANES
    image[:, whole:] = jnp.zeros((image.shape[0], image.shape[1] - whole), jnp.float32)

    def line(i, value, following, preceding):
        weight = weights[i]
        east = jnp.concatenate([value[1:], right[pl.ds(i, 1)]], axis=0)
        west = jnp.concatenate([left[pl.ds(i, 1)], value[:-1]], axis=0)
        flux = weight[:, 0:1] * (east - value) + weight[:, 1:2] * (west - value)
        flux = flux + weight[:, 2:3] * (following - value) + weight[:, 3:4] * (preceding - value)
        image[pl.ds(pl.multiple_of(i * lons, lons), lons), :width] = value + rate * flux

    line(0, field[0], field[1], before[...])
    line(lats - 1, field[lats - 1], after[...], field[lats - 2])

    def inner(i, state):
        line(i, field[i], field[i + 1], field[i - 1])
        return state

    over_lines(lats, inner, 0)

    for (side, live), out in zip(live_counts(counts), (own, other)):

        @pl.loop(0, (live + 15) // 16)
        def _(j):
            base = pl.multiple_of(j * 16, 16)
            lines = [image[pl.ds(cells[side, base + k], 1)] for k in range(16)]
            out[pl.ds(base, 16)] = jnp.concatenate(lines, axis=0)


def scatter_kernel(own, other, weights, rates, cells, counts, spread, to_before, to_after, to_left, to_right, *parts):
    lats, lons, _ = weights.shape
    width = rates.shape[1]
    rate = rates[...]
    for part in parts:
        part[...] = jnp.zeros_like(part)
    for (side, live), grads in zip(live_counts(counts), (own, other)):

        @pl.loop(0, (live + len(parts) - 1) // len(parts))
        def _(j):
            base = j * len(parts)
            places = [pl.ds(cells[side, base + k], 1) for k in range(len(parts))]
            sums = []
            for k, (part, place) in enumerate(zip(parts, places)):
                term = jnp.where(base + k < live, grads[pl.ds(base + k, 1)], 0.0)
                sums.append(part[place] + term)
            for part, place, total in zip(parts, places, sums):
                part[place] = total

    block = 8 * lons

    @pl.loop(0, spread.shape[0] // block)
    def _(j):
        lines = pl.ds(pl.multiple_of(j * block, block), block)
        spread[lines] = (parts[0][lines] + parts[1][lines]) + (parts[2][lines] + parts[3][lines])

    to_before[...] = weights[0][:, 3:4] * (rate * spread[:lons, :width])
    to_after[...] = weights[lats - 1][:, 2:3] * (rate * spread[(lats - 1) * lons :, :width])

    @pl.loop(0, lats // 8)
    def _(j):
        starts, ends = [], []
        for k in range(8):
            i = j * 8 + k
            base = pl.multiple_of(i * lons, lons)
            weight = weights[i]
            starts.append(weight[:1, 1:2] * (rate * spread[pl.ds(base, 1), :width]))
            ends.append(weight[lons - 1 :, 0:1] * (rate * spread[pl.ds(base + lons - 1, 1), :width]))
        lines = pl.ds(pl.multiple_of(j * 8, 8), 8)
        to_left[lines] = jnp.concatenate(starts, axis=0)
        to_right[lines] = jnp.concatenate(ends, axis=0)


def adjoint_kernel(is_first, spread, before, after, left, right, weights, rates, field, sums, out, *rest):
    lats, lons, width = field.shape
    rate = rates[...]

    def scaled(i):
        return rate * spread[pl.ds(pl.multiple_of(i * lons, lons), lons), :width]

    def line(i, preceding, following, totals):
        weight = weights[i]
        value = spread[pl.ds(pl.multiple_of(i * lons, lons), lons), :width]
        flow = rate * value
        east = weight[:, 0:1] * flow
        west = weight[:, 1:2] * flow
        total = weight[:, 0:1] + weight[:, 1:2] + weight[:, 2:3] + weight[:, 3:4]
        result = value - total * flow + preceding + following
        result = result + jnp.concatenate([left[pl.ds(i, 1)], east[:-1]], axis=0)
        result = result + jnp.concatenate([west[1:], right[pl.ds(i, 1)]], axis=0)
        out[i] = result
        known = field[i]
        if not is_first:
            return (totals[0] + known * result,)
        rest[2][pl.ds(i, 1)] = result[:1]
        rest[3][pl.ds(i, 1)] = result[lons - 1 :]
        return totals[0] + known * known, totals[1] + known * result, totals[2] + result * result

    def inner(i, totals):
        return line(i, weights[i - 1][:, 2:3] * scaled(i - 1), weights[i + 1][:, 3:4] * scaled(i + 1), totals)

    totals = tuple(jnp.zeros((lons, width), jnp.float32) for _ in range(3 if is_first else 1))
    totals = line(0, before[...], weights[1][:, 3:4] * scaled(1), totals)
    totals = over_lines(lats, inner, totals)
    totals = line(lats - 1, weights[lats - 2][:, 2:3] * scaled(lats - 2), after[...], totals)
    lines = lax.broadcasted_iota(jnp.int32, sums.shape, 0)
    block = sums[...]
    for k, total in enumerate(totals):
        block = jnp.where(lines == (k if is_first else 3), jnp.sum(total), block)
    if is_first:
        rest[0][...] = out[0]
        rest[1][...] = out[lats - 1]
    rest[-1][...] = block


def split_kernel(wide, w_own, w_other, w_mid, w_out, cov, *outs):
    pairs = [outs[2 * k : 2 * k + 2] for k in range(4)]
    scale_out = outs[8]
    for pair in (pairs[0], pairs[2], pairs[3]):
        for half in pair:
            half[...] = jnp.zeros_like(half)
    chunk = 32

    def squares(full, pair, base):
        high, low = pair
        rows, columns = full.shape

        def store(start, value):
            lines = pl.ds(start, chunk)
            rounded = value.astype(jnp.bfloat16)
            high[lines, :columns] = rounded
            low[lines, :columns] = (value - rounded.astype(jnp.float32)).astype(jnp.bfloat16)
            square = value * value
            return (square[:8] + square[8:16]) + (square[16:24] + square[24:])

        def split(c, total):
            start = pl.multiple_of(c * chunk, chunk)
            return total + store(pl.multiple_of(base + start, chunk), full[pl.ds(start, chunk)])

        total = lax.fori_loop(0, rows // chunk, split, jnp.zeros((8, columns), jnp.float32))
        left = rows % chunk
        if left:
            rest = jnp.concatenate([full[rows - left :], jnp.zeros((chunk - left, columns), jnp.float32)], axis=0)
            total = total + store(base + rows - left, rest)
        return jnp.sum(total, axis=(0, 1), keepdims=True)

    first = squares(w_own, pairs[0], 0) + squares(w_other, pairs[0], wide)
    bound = first * squares(w_mid, pairs[1], 0) * squares(w_out, pairs[2], 0)
    scale = 1.0 / jnp.maximum(bound * jnp.sqrt(squares(cov, pairs[3], 0)), 1.0)
    scale_out[...] = jnp.broadcast_to(scale, scale_out.shape)


def network_kernel(own, other, gate_one, gate_two, *rest):
    p_in, p_mid, p_out, p_cov = (rest[2 * k : 2 * k + 2] for k in range(4))
    scale, counts, d_own, d_other = rest[8:]
    factor = scale[0:1, 0:1]
    wide = own.shape[1]

    def product(value, pair, back=False):
        dims = (((1,), (1 if back else 0,)), ((), ()))
        high = value.astype(jnp.bfloat16)
        low = (value - high.astype(jnp.float32)).astype(jnp.bfloat16)

        def dot(left, right):
            return lax.dot_general(left, right[...], dims, preferred_element_type=jnp.float32)

        count = value.shape[0]
        both = dot(jnp.concatenate([high, low], axis=0), pair[0])
        return both[:count] + (both[count:] + dot(high, pair[1]))

    rows = min(256, own.shape[0])
    live = live_counts(counts)[0][1]

    @pl.loop(0, (live + rows - 1) // rows)
    def _(j):
        lines = pl.ds(pl.multiple_of(j * rows, rows), rows)
        columns = jnp.concatenate([own[lines], other[lines]], axis=1)
        hidden = product(columns, p_in) * gate_one[lines].astype(jnp.float32)
        hidden = product(hidden, p_mid) * gate_two[lines].astype(jnp.float32)
        weighted = product(product(hidden, p_out, True), p_cov) * factor
        back = product(weighted, p_out) * gate_two[lines].astype(jnp.float32)
        back = product(back, p_mid, True) * gate_one[lines].astype(jnp.float32)
        terms = product(back, p_in, True)
        d_own[lines] = terms[:, :wide]
        d_other[lines] = terms[:, wide:]


def combination(scale, bb, bw, ww, wx):
    bw = bw / scale
    curve = bb + bw
    step = bb / curve
    rest = bw / curve
    grown = step / scale
    ratio = (grown * ww / bb) * grown - rest * rest
    norm = ratio * bb
    along = norm + rest * rest * bw - 2.0 * rest * (grown * ww / scale) + grown * (grown * wx) / scale
    second = norm / (along - ratio * norm / step)
    mixed = rest + ratio
    of_solution = (step + second * mixed, -second * grown)
    of_residual = (
        rest - second * mixed,
        -grown - second * (mixed / scale - grown),
        (second / scale) * grown,
    )
    return of_solution, of_residual


def finish_kernel(sums, scale, b, w, x, solution, residual):
    values = [sums[k : k + 1, 0:1] for k in range(4)]
    of_solution, of_residual = combination(scale[0:1, 0:1], *values)
    solution[...] = of_solution[0] * b[...] + of_solution[1] * w[...]
    residual[...] = of_residual[0] * b[...] + of_residual[1] * w[...] + of_residual[2] * x[...]


def finish(sums, scale, b, w, x):
    lats, lons, width = b.shape
    part = 8 if lats % 8 == 0 else lats
    whole = pl.BlockSpec(sums.shape, lambda i: (0, 0))
    block = pl.BlockSpec((part, lons, width), lambda i: (i, 0, 0))
    return pl.pallas_call(
        finish_kernel,
        grid=(lats // part,),
        out_shape=[jax.ShapeDtypeStruct(b.shape, jnp.float32)] * 2,
        in_specs=[whole, whole, block, block, block],
        out_specs=[block, block],
        compiler_params=pltpu.CompilerParams(vmem_limit_bytes=24 * MIB),
    )(sums, scale, b, w, x)


def swapped(value):
    return lax.ppermute(value, "side", [(0, 1), (1, 0)])


def local(
    right_side,
    couplings,
    channel_rates,
    weight_in,
    weight_mid,
    weight_out,
    inverse_cov,
    profile_cells,
    profile_counts,
    gate_first,
    gate_second,
):
    side = lax.axis_index("side")
    lats, lons, width = right_side.shape
    slots = profile_cells.shape[1]
    wide = -(-width // LANES) * LANES
    channels = -(-weight_out.shape[1] // LANES) * LANES
    latitude = lax.axis_index("row") * lats + jnp.arange(lats)
    north_open = (latitude < lats * lax.axis_size("row") - 1)[:, None]
    south_open = (latitude > 0)[:, None]
    weights = jnp.stack(
        [
            couplings[0],
            couplings[1],
            jnp.where(north_open, couplings[2], 0.0),
            jnp.where(south_open, couplings[3], 0.0),
        ],
        axis=2,
    )
    rates = channel_rates.reshape(1, width)
    halves = [lax.dynamic_slice_in_dim(weight_in, part * width, width, 0) for part in (side, 1 - side)]
    hidden = weight_in.shape[1]
    hidden = weight_in.shape[1]
    matrices = (*halves, weight_mid, weight_out.T, inverse_cov)
    shapes = [(2 * wide, hidden), (hidden, hidden), (channels, hidden), (channels, channels)]
    shapes = [(*shape, "half") for shape in shapes for _ in range(2)] + [(8, LANES)]
    *pairs, scale = call(functools.partial(split_kernel, wide), 28, shapes, [VMEM] * 5, [], *matrices)
    lat_edge, lon_edge = (lons, width), (lats, width)

    def spread(field, edges, known, sums, is_first):
        around = halos(*edges)
        image = [pltpu.VMEM((lats * lons, wide), jnp.float32)]
        specs = [VMEM] * 7 + [SMEM] * 2
        operands = (field, *around, weights, rates, profile_cells, profile_counts)
        own, other = call(gather_kernel, 16, [(slots, wide)] * 2, specs, image, *operands)
        other = swapped(other)
        operands = (own, other, gate_first, gate_second, *pairs, scale, profile_counts)
        own, other = call(network_kernel, 36, [(slots, wide)] * 2, [VMEM] * 13 + [SMEM], [], *operands)
        other = swapped(other)
        parts = [pltpu.VMEM((lats * lons, wide), jnp.float32)] * 4
        shapes = [(lats * lons, wide), lat_edge, lat_edge, lon_edge, lon_edge]
        operands = (own, other, weights, rates, profile_cells, profile_counts)
        summed, *edges = call(scatter_kernel, 24, shapes, [VMEM] * 4 + [SMEM] * 2, parts, *operands)
        around = halos(*edges)
        shapes = [field.shape] + ([lat_edge, lat_edge, lon_edge, lon_edge] if is_first else []) + [(8, LANES)]
        operands = (summed, *around, weights, rates, known, sums)
        out, *edges, sums = call(functools.partial(adjoint_kernel, is_first), 16, shapes, [VMEM] * 9, [], *operands)
        return out, edges, sums

    edges = (right_side[0], right_side[lats - 1], right_side[:, 0], right_side[:, lons - 1])
    first, edges, sums = spread(right_side, edges, right_side, jnp.zeros((8, LANES), jnp.float32), True)
    second, _, sums = spread(first, edges, first, sums, False)
    return tuple(finish(all_sums(sums), scale, right_side, first, second))


def solution(mesh):
    in_specs = (
        P("row", "col", "side"),
        P(None, "row", "col"),
        P("side"),
        P(),
        P(),
        P(),
        P(),
        P(None, ("row", "col")),
        P(),
        P(("side", "row", "col"), None),
        P(("side", "row", "col"), None),
    )
    out_specs = (P("row", "col", "side"), P("row", "col", "side"))
    return jax.shard_map(local, mesh=mesh, in_specs=in_specs, out_specs=out_specs, check_vma=False)
```
